512 devices in a mesh: expert: 64 (over y, z), tensor: 8 (over x, core).
Axes of the slice: x: 4, y: 8, z: 8, core: 2. Of those that a mesh axis runs over, the one named last changes fastest.
Arguments:
- queries: bfloat16 [8192, 4096], P('expert', 'tensor'), may hold values from -6 to 6
- keys: bfloat16 [8192, 512], P('expert'), may hold values from -6 to 6
- values: bfloat16 [8192, 512], P('expert'), may hold values from -6 to 6
- segments: int32 [64, 128], P('expert'), may hold values from 0 to 3, never falling along the last dimension, each value on 1 to 64 neighbouring positions
- out_weight: bfloat16 [4096, 2048], P('tensor'), may hold values from -0.09375 to 0.09375
- residual: bfloat16 [8192, 2048], P(('expert', 'tensor')), may hold values from -4 to 4
- norm_gain: float32 [2048], replicated, may hold values from 0.1 to 1.9
- picks: int32 [8192, 8], P('expert'), may hold values from 0 to 63, all different within a row; in each aligned block of 16 rows (0 to 15, 16 to 31, ...) at most 3 rows name the same one
- route_weights: float32 [8192, 8], P('expert'), may hold values from 0.1 to 0.5
- w_gate: bfloat16 [64, 2048, 1536], P('expert', None, 'tensor'), may hold values from -0.125 to 0.125
- w_up: bfloat16 [64, 2048, 1536], P('expert', None, 'tensor'), may hold values from -0.125 to 0.125
- w_down: bfloat16 [64, 1536, 2048], P('expert', None, 'tensor'), may hold values from -0.15625 to 0.15625
Outputs:
- stream: bfloat16 [8192, 2048], P(('expert', 'tensor'))
- layer_out: bfloat16 [8192, 2048], P(('expert', 'tensor'))
The draws below stay inside these ranges and needn't reach their ends.
Inputs may be any that keep to these rules, and one draw needn't show every extreme that they name: A token's 8 picks are distinct. Split the tokens into aligned blocks of 16 rows; in each block no expert is picked by more than 3 rows.
All inputs are finite; a program needn't handle non-finite values.
Results may differ from the reference program's by a relative error of at most 0.02.
Values may be sent and summed in bfloat16 or wider, within the bound.
A program may use at most 64 MiB of HBM per device.

```python
import math
import jax
import jax.numpy as jnp
import numpy as np
from jax import lax

D = 2048
HEADS = 32
KVH = 4
HD = 128
FFE = 1536
TOP = 8
DOCS = 4
TOKG = 128
EXPERTS = 64
GROUPS = 64
TOKENS = 8192
ROWS = 16
CAP = 3
N_TENSOR = 8


def draw_queries(key, part):
    key = jax.random.fold_in(key, 11)
    result = jnp.clip(jax.random.normal(key, (TOKENS, HEADS, HD), jnp.float32), -6.0, 6.0)
    return result.reshape(TOKENS, HEADS * HD).astype(jnp.bfloat16)


def draw_keys(key, part):
    key = jax.random.fold_in(key, 12)
    result = jnp.clip(jax.random.normal(key, (TOKENS, KVH, HD), jnp.float32), -6.0, 6.0)
    return result.reshape(TOKENS, KVH * HD).astype(jnp.bfloat16)


def draw_residual(key, part):
    key = jax.random.fold_in(key, 13)
    column_key = jax.random.fold_in(key, 0)
    entry_key = jax.random.fold_in(key, 2)
    column_scale = 10.0 ** jax.random.uniform(column_key, (D,), jnp.float32, -1.0, 0.0)
    entries = jnp.clip(jax.random.normal(entry_key, (TOKENS, D), jnp.float32), -4.0, 4.0)
    return (entries * column_scale[None, :]).astype(jnp.bfloat16)


def block_levels(own_key, extent, shards, low, top_value):
    factor_of = 1.0
    for dim, blocks in shards:
        steps = jax.random.uniform(jax.random.fold_in(jax.random.fold_in(own_key, 6), dim), (blocks,), jnp.float32, low / len(shards), top_value / len(shards))
        factor_of = factor_of * jnp.repeat(jnp.exp(steps), extent[dim] // blocks).reshape((-1,) + (1,) * (len(extent) - 1 - dim))
    return factor_of


def length_profile(number_of, total, most, skew):
    weights = [(1 << 20) // math.isqrt(standing ** skew) + 1 for standing in range(2, number_of + 1)]
    spare, holding = total - most - (number_of - 1), [1] * (number_of - 1)
    while spare > 0:
        candidates = [i for i in range(number_of - 1) if holding[i] < most]
        mass, remaining = sum([weights[i] for i in candidates]), spare
        for i in candidates:
            more = min(most - holding[i], max(1, remaining * weights[i] // mass), spare)
            holding[i] = holding[i] + more
            spare = spare - more
    return np.array([most] + holding)


def uneven(rng, amount, total, reach, lean):
    if amount == 2:
        one = jax.random.randint(rng, (), max(1, total - reach), min(reach, total - 1) + 1)
        return jnp.stack([one, total - one])
    tallies = jnp.asarray(length_profile(amount, total, reach, lean), jnp.int32)
    couples = (amount - 1) // 2
    giver, taker = tallies[1:1 + 2 * couples:2], tallies[2:2 + 2 * couples:2]
    margin = jnp.minimum(giver - 1, reach - taker)
    moved = jax.random.randint(jax.random.fold_in(rng, 1), (couples,), 0, 1 << 20) % (margin + 1)
    tallies = tallies.at[1:1 + 2 * couples:2].set(giver - moved).at[2:2 + 2 * couples:2].set(taker + moved)
    return tallies[jax.random.permutation(jax.random.fold_in(rng, 2), amount)]


def deal_out(stream_key, own, number, rows, count, top, reach, lean):
    sequence = jax.random.permutation(stream_key, count)
    crowded, usual = shares(count, rows * top, reach, lean, True), shares(count, rows * top, reach, lean, False)
    places = jnp.arange(count)

    def named(lengths, turn):
        used = int((lengths > 0).sum())
        fixed = max(1, used // 4)
        moved = fixed + (places - fixed + turn * (used - fixed)) % max(1, count - fixed)
        return jnp.zeros((count,), jnp.int32).at[sequence[jnp.where(places < fixed, places, moved)]].set(jnp.asarray(lengths, jnp.int32))

    lengths = jnp.where(number % 4 == 0, named(crowded, number // 4), named(usual, number - number // 4 - 1))
    mixed = jax.random.permutation(jax.random.fold_in(own, 3), count)
    donor, sink = mixed[0:count // 2 * 2:2], mixed[1:count // 2 * 2:2]
    room = jnp.minimum(lengths[donor] - 1, reach - lengths[sink]) // 2
    room = jnp.where((donor == sequence[0]) | (sink == sequence[0]) | (lengths[sink] == 0), 0, jnp.maximum(room, 0))
    moved = jax.random.randint(jax.random.fold_in(own, 4), (count // 2,), 0, 1 << 20) % (room + 1)
    lengths = lengths.at[donor].add(-moved).at[sink].add(moved)
    members = jnp.searchsorted(jnp.cumsum(lengths), jnp.arange(rows * top), side="right").astype(jnp.int32)
    table = members.reshape(top, rows).T
    table = table[jax.random.permutation(jax.random.fold_in(own, 1), rows)]
    turn = jax.random.randint(jax.random.fold_in(own, 2), (rows, 1), 0, top)
    return jnp.take_along_axis(table, (jnp.arange(top)[None, :] + turn) % top, axis=1)


def shares(count, total, limit, lean, full):
    loads = [(1 << 20) // math.isqrt(grade ** lean) + 1 for grade in range(1, count + 1)]
    largest = limit if full else min(limit, max(-(-total // count), total * loads[0] // sum(loads)))
    least = 1 if total - largest >= count - 1 else 0
    given, surplus = [largest] + [least] * (count - 1), total - largest - least * (count - 1)
    while surplus > 0:
        candidates = [i for i in range(1, count) if given[i] < largest] or [i for i in range(1, count) if given[i] < limit]
        whole, budget = sum([loads[i] for i in candidates]), surplus
        for i in candidates:
            more = min(limit - given[i], max(1, budget * loads[i] // whole), surplus)
            given[i] = given[i] + more
            surplus = surplus - more
    return np.array(given)


def noise(rng, shape, spread, limit, cuts=(), held_as=jnp.bfloat16):
    level = block_levels(rng, shape, cuts, -0.22, 0.18) if cuts else 1.0
    values = jax.random.normal(rng, shape, jnp.float32) * spread * level
    return jnp.minimum(jnp.maximum(values, -limit), limit).astype(held_as)


def setup_inputs(seed: int = 0) -> dict:
    arg_keys = jax.random.split(jax.random.key(seed), 13)
    queries = draw_queries(jax.random.fold_in(arg_keys[12], 71), 0)
    keys = draw_keys(jax.random.fold_in(arg_keys[12], 71), 0)
    values = noise(arg_keys[2], (TOKENS, KVH * HD), 1.0, 6.0, ((0, 64),))
    segments = jax.vmap(lambda own: jnp.searchsorted(jnp.cumsum(uneven(own, DOCS, TOKG, TOKG // 2, 2)), jnp.arange(TOKG), side="right"))(jax.random.split(arg_keys[3], GROUPS)).reshape((GROUPS, TOKG)).astype(jnp.int32)
    out_weight = noise(arg_keys[4], (HEADS * HD, D), (HEADS * HD) ** -0.5, 0.09375, ((0, 8),))
    residual = draw_residual(jax.random.fold_in(arg_keys[12], 71), 0)
    norm_gain = jnp.clip(1.0 + 0.18 * jax.random.normal(arg_keys[6], (D,), jnp.float32), 0.1, 1.9)
    picks_keys = jax.random.split(jax.random.fold_in(arg_keys[7], 1), TOKENS // ROWS)
    picks_turns = jax.random.permutation(jax.random.fold_in(arg_keys[7], 3), TOKENS // ROWS)
    picks = jax.vmap(lambda own, number: deal_out(jax.random.fold_in(arg_keys[7], 2), own, number, ROWS, EXPERTS, TOP, CAP, 2))(picks_keys, picks_turns).reshape((TOKENS, TOP))
    route_weights = jnp.clip(0.1 + 0.4 * jax.random.uniform(arg_keys[8], (TOKENS, TOP), jnp.float32) ** block_levels(arg_keys[8], (TOKENS, TOP), ((0, 64),), -0.2, 0.2), 0.1, 0.5)
    w_gate = noise(arg_keys[9], (EXPERTS, D, FFE), D ** -0.5, 0.125, ((0, 64), (2, 8)))
    w_up = noise(arg_keys[10], (EXPERTS, D, FFE), D ** -0.5, 0.125, ((0, 64), (2, 8)))
    w_down = noise(arg_keys[11], (EXPERTS, FFE, D), FFE ** -0.5, 0.15625, ((0, 64), (2, 8)))
    return {"queries": queries, "keys": keys, "values": values, "segments": segments, "out_weight": out_weight, "residual": residual, "norm_gain": norm_gain, "picks": picks, "route_weights": route_weights, "w_gate": w_gate, "w_up": w_up, "w_down": w_down}


def attend(inputs, out_weight):
    queries, keys, values, documents = inputs
    query_heads = queries.reshape(TOKG, HEADS, HD).astype(jnp.float32)
    key_heads = jnp.repeat(keys.reshape(TOKG, KVH, HD).astype(jnp.float32), HEADS // KVH, axis=1)
    value_heads = jnp.repeat(values.reshape(TOKG, KVH, HD).astype(jnp.float32), HEADS // KVH, axis=1)
    scores = jnp.einsum('thd,shd->hts', query_heads, key_heads) * (1.0 / math.sqrt(HD))
    position = jnp.arange(TOKG, dtype=jnp.int32)
    visible = (documents[:, None] == documents[None, :]) & (position[None, :] <= position[:, None])
    scores = jnp.where(visible[None], scores, -1e+30)
    row_top = lax.optimization_barrier(jnp.max(scores, axis=2, keepdims=True))
    expanded = jnp.exp(scores - row_top)
    weights_bf = (expanded / lax.optimization_barrier(jnp.sum(expanded, axis=2, keepdims=True))).astype(jnp.bfloat16)
    context = jnp.einsum('hts,shd->thd', weights_bf.astype(jnp.float32), value_heads).astype(jnp.bfloat16)
    block_width = HEADS * HD // N_TENSOR
    context_blocks = context.reshape(TOKG, N_TENSOR, block_width).astype(jnp.float32)
    weight_blocks = out_weight.reshape(N_TENSOR, block_width, D).astype(jnp.float32)
    partials = jnp.einsum('tnk,nkd->ntd', context_blocks, weight_blocks).astype(jnp.bfloat16)
    return lax.optimization_barrier(jnp.sum(partials.astype(jnp.float32), axis=0))

def reference(queries, keys, values, segments, out_weight, residual, norm_gain, picks, route_weights, w_gate, w_up, w_down):
    grouped = (queries.reshape(GROUPS, TOKG, HEADS * HD), keys.reshape(GROUPS, TOKG, KVH * HD), values.reshape(GROUPS, TOKG, KVH * HD), segments)
    attended = lax.map(lambda inputs: attend(inputs, out_weight), grouped).reshape(TOKENS, D)
    hidden_sum = residual.astype(jnp.float32) + attended
    stream = hidden_sum.astype(jnp.bfloat16)
    mean_square = lax.optimization_barrier(jnp.mean(hidden_sum * hidden_sum, axis=1, keepdims=True))
    normed = (hidden_sum * lax.rsqrt(mean_square + 1e-06) * norm_gain[None, :]).astype(jnp.bfloat16)
    most_rows = TOKENS // ROWS * CAP

    def expert_step(running, inputs):
        number, gate_weight, up_weight, down_weight = inputs
        chosen = picks == number
        weight = lax.optimization_barrier(jnp.sum(jnp.where(chosen, route_weights, jnp.zeros_like(route_weights)), axis=1))
        picked_rows = jnp.any(chosen, axis=1)
        row_list = jnp.nonzero(picked_rows, size=most_rows, fill_value=0)[0].astype(jnp.int32)
        living = (jnp.arange(most_rows, dtype=jnp.int32) < jnp.sum(picked_rows.astype(jnp.int32))).astype(weight.dtype)
        gathered = normed[row_list]
        gate_value = jnp.dot(gathered, gate_weight, preferred_element_type=jnp.float32)
        up_value = jnp.dot(gathered, up_weight, preferred_element_type=jnp.float32)
        active = (jax.nn.silu(gate_value) * up_value).astype(jnp.bfloat16)
        expert_out = jnp.dot(active, down_weight, preferred_element_type=jnp.float32).astype(jnp.bfloat16)
        weighted = expert_out.astype(jnp.float32) * (weight[row_list] * living)[:, None]
        return (running.at[row_list].add(weighted), None)
    mixture, _ = lax.scan(expert_step, jnp.zeros((TOKENS, D), jnp.float32), (jnp.arange(EXPERTS, dtype=jnp.int32), w_gate, w_up, w_down))
    layer_out = (hidden_sum + mixture).astype(jnp.bfloat16)
    return (stream, layer_out)
```

```python
import math

import jax
import jax.numpy as jnp
from jax import lax
from jax.experimental import pallas as pl
from jax.experimental.pallas import tpu as pltpu
from jax.sharding import PartitionSpec as P

D = 2048
HEADS = 32
KVH = 4
HD = 128
TOP = 8
ROWS = 16
CAP = 3
XN = 4
RING = 8
QD = D // XN
HID = 192
BLKS = RING * XN
HALF = CAP * BLKS // 2
SLOTS = 2 * HALF
TOKS = BLKS * ROWS
BF = jnp.bfloat16
F32 = jnp.float32


def ahead(step):
    odd = lax.rem(step, 2)
    return RING + odd * ((step + 1) // 2) - (1 - odd) * (step // 2)


def moe_kernel(
    nrm, hid, meta, wg, wu, wd,
    out,
    wgs, wus, wds, metas, gath, code, wtok, table, wflat, comb, disp, xg, act, back, ret, part, parts, mix, fin,
    w_s, w_r, m_s, m_r, xa_s, xa_r, g_s, g_r, d_s, d_r, xg_s, xg_r, ac_s, ac_r, rt_s, rt_r, rs_s, rs_r, xb_s, xb_r,
):
    exp = lax.axis_index("expert")
    ten = lax.axis_index("tensor")
    x = ten // 2
    c = lax.rem(ten, 2)
    y = exp // RING
    z = lax.rem(exp, RING)
    st1 = RING - (RING - 1) * c
    st2 = 1 + (RING - 1) * c
    r1 = (1 - c) * y + c * z
    r2 = (1 - c) * z + c * y

    def ring1(r):
        return r * st1 + r2 * st2, ten

    def ring2(r):
        return r1 * st1 + r * st2, ten

    def along_x(xx):
        return exp, xx * 2 + c

    sibling = (exp, x * 2 + 1 - c)
    xp = lax.rem(x + 1, XN)
    xm = lax.rem(x + XN - 1, XN)
    xo = lax.rem(x + 2, XN)

    def rcopy(src, dst, ss, rs, dev):
        return pltpu.make_async_remote_copy(
            src_ref=src, dst_ref=dst, send_sem=ss, recv_sem=rs, device_id=dev,
            device_id_type=pl.DeviceIdType.MESH,
        )

    def arrived(dst, rs):
        rcopy(dst, dst, rs, rs, sibling).wait_recv()

    def sent(src, ss):
        rcopy(src, src, ss, ss, sibling).wait_send()

    def band(xx, width):
        return pl.ds(pl.multiple_of(xx * width, 128), width)

    def block(xx):
        return pl.ds(pl.multiple_of(xx * ROWS, ROWS), ROWS)

    barrier = pltpu.get_barrier_semaphore()

    def greet(dev):
        pl.semaphore_signal(barrier, inc=1, device_id=dev, device_id_type=pl.DeviceIdType.MESH)

    greet(sibling)
    for d in range(1, XN):
        greet(along_x(lax.rem(x + d, XN)))
    for d in range(1, RING):
        greet(ring1(lax.rem(r1 + d, RING)))
        greet(ring2(lax.rem(r2 + d, RING)))
    pl.semaphore_wait(barrier, 1 + (XN - 1) + 2 * (RING - 1))

    for d in range(1, XN):
        to = lax.rem(x + d, XN)
        rcopy(nrm.at[:, band(to, QD)], gath.at[r1, block(x)], xa_s.at[d], xa_r.at[d], along_x(to)).start()
    gath[r1, block(x), :] = nrm[:, band(x, QD)]
    for d in range(1, RING):
        to = lax.rem(r1 + d, RING)
        rcopy(meta, metas.at[r1], m_s.at[d], m_r.at[d], ring1(to)).start()
    metas[r1] = meta[...]
    for d in range(1, XN):
        arrived(gath.at[r1, block(lax.rem(x + XN - d, XN))], xa_r.at[d])
    for d in range(1, RING):
        to = lax.rem(r1 + d, RING)
        rcopy(gath.at[r1], gath.at[r1], g_s.at[d], g_r.at[d], ring1(to)).start()
    for k, (mine, theirs) in enumerate(((wg, wgs), (wu, wus), (wd, wds))):
        rcopy(mine, theirs, w_s.at[k], w_r.at[k], sibling).start()

    for d in range(1, RING):
        arrived(metas.at[lax.rem(r1 + RING - d, RING)], m_r.at[d])
    ids = (r1 * st1 + lax.broadcasted_iota(jnp.int32, (RING, 128), 0) * st2).astype(F32)
    row_a = lax.broadcasted_iota(jnp.int32, (128, 128), 0)
    row_b = lax.broadcasted_iota(jnp.int32, (128, 128), 1)
    before = ((row_a // ROWS == row_b // ROWS) & (row_a < row_b)).astype(F32).astype(BF)
    low = lax.broadcasted_iota(jnp.int32, (2 * TOP, 128), 1) < 64
    for p in range(RING // 2):
        pair = jnp.where(low, metas[2 * p], metas[2 * p + 1])
        member = jnp.zeros((RING, 128), F32)
        weight = jnp.zeros((RING, 128), F32)
        for k in range(TOP):
            hit = pair[k : k + 1, :] == ids
            member = member + hit.astype(F32)
            weight = weight + jnp.where(hit, pair[TOP + k : TOP + k + 1, :], 0.0)
        rank = jnp.dot(member.astype(BF), before, preferred_element_type=F32)
        code[:, p * 128 : (p + 1) * 128] = jnp.where(member > 0.5, rank, -1.0)
        wtok[:, p * 128 : (p + 1) * 128] = weight
    slot = lax.broadcasted_iota(jnp.int32, (HALF, TOKS // 2), 0)
    token = lax.broadcasted_iota(jnp.int32, (HALF, TOKS // 2), 1)
    same = lax.rem(slot, BLKS // 2) == token // ROWS
    place = jnp.where(same, (slot // (BLKS // 2)).astype(F32), -2.0)
    for h in range(2):
        lanes = slice(h * (TOKS // 2), (h + 1) * (TOKS // 2))
        for e in range(RING):
            mask = place == code[e : e + 1, lanes]
            table[e, h] = mask.astype(F32).astype(BF)
            wflat[e * HALF : (e + 1) * HALF, :] = jnp.where(mask, wtok[e : e + 1, lanes], 0.0)
        turned = wflat[...].T
        coarse = turned.astype(BF)
        comb[h, : TOKS // 2] = coarse
        comb[h, TOKS // 2 :] = (turned - coarse.astype(F32)).astype(BF)

    for d in range(1, RING):
        arrived(gath.at[lax.rem(r1 + RING - d, RING)], g_r.at[d])

    def slots_for(e):
        tops = []
        for h in range(2):
            rows = gath[h * (RING // 2) : (h + 1) * (RING // 2)].reshape(TOKS // 2, QD)
            tops.append(jnp.dot(table[e, h], rows, preferred_element_type=F32).astype(BF))
        return tops

    def spread(ref, sem_s, sem_r, i, width):
        piece = ref.at[i, :, band(x, width)]
        rcopy(piece, piece, sem_s.at[i, 0], sem_r.at[i, 0], along_x(xp)).start()
        rcopy(piece, piece, sem_s.at[i, 1], sem_r.at[i, 1], along_x(xm)).start()

    def relay(ref, sem_s, sem_r, i, width):
        arrived(ref.at[i, :, band(xm, width)], sem_r.at[i, 0])
        up = ref.at[i, pl.ds(0, HALF), band(xm, width)]
        rcopy(up, up, sem_s.at[i, 2], sem_r.at[i, 2], along_x(xp)).start()
        arrived(ref.at[i, :, band(xp, width)], sem_r.at[i, 1])
        down = ref.at[i, pl.ds(HALF, HALF), band(xp, width)]
        rcopy(down, down, sem_s.at[i, 3], sem_r.at[i, 3], along_x(xm)).start()

    def relayed(ref, sem_r, i, width):
        arrived(ref.at[i, pl.ds(0, HALF), band(xo, width)], sem_r.at[i, 2])
        arrived(ref.at[i, pl.ds(HALF, HALF), band(xo, width)], sem_r.at[i, 3])

    own = slots_for(r2)
    for h in range(2):
        xg[0, h * HALF : (h + 1) * HALF, band(x, QD)] = own[h]
    spread(xg, xg_s, xg_r, 0, QD)

    def dispatch(i, carry):
        to = lax.rem(r2 + ahead(i), RING)
        tops = slots_for(to)
        for h in range(2):
            disp[i, h * HALF : (h + 1) * HALF, :] = tops[h]
        rcopy(disp.at[i], xg.at[i, :, band(x, QD)], d_s.at[i], d_r.at[i], ring2(to)).start()
        return carry

    lax.fori_loop(1, RING, dispatch, 0)

    for k, theirs in enumerate((wgs, wus, wds)):
        arrived(theirs, w_r.at[k])

    def gate_up(i):
        relayed(xg, xg_r, i, QD)
        rows = xg[i]

        def units(gate, up):
            g = jnp.dot(rows, gate[...], preferred_element_type=F32)
            u = jnp.dot(rows, up[...], preferred_element_type=F32)
            return g / (1.0 + jnp.exp(-g)) * u

        mine = units(wg, wu)
        theirs = units(wgs, wus)
        first = jnp.where(c == 0, mine, theirs)
        second = jnp.where(c == 0, theirs, mine)
        act[i, :, band(x, 2 * HID)] = jnp.concatenate([first, second], axis=1).astype(BF)
        spread(act, ac_s, ac_r, i, 2 * HID)

    def down(i):
        relayed(act, ac_r, i, 2 * HID)
        rows = act[i]
        mine = jnp.dot(rows, wd[...], preferred_element_type=F32).astype(BF)
        theirs = jnp.dot(rows, wds[...], preferred_element_type=F32).astype(BF)
        back[i, :, band(c, QD // 2)] = mine
        back[i, :, band(1 - c, QD // 2)] = theirs

        @pl.when(i == 0)
        def _():
            ret[r2] = back[0]

        @pl.when(i > 0)
        def _():
            to = lax.rem(r2 + 2 * RING - ahead(i), RING)
            rcopy(back.at[i], ret.at[r2], rt_s.at[i], rt_r.at[i], ring2(to)).start()

    def step(it, carry):
        @pl.when(it < RING - 1)
        def _():
            arrived(xg.at[it + 1, :, band(x, QD)], d_r.at[it + 1])
            spread(xg, xg_s, xg_r, it + 1, QD)

        @pl.when(it < RING)
        def _():
            relay(xg, xg_s, xg_r, it, QD)

        @pl.when((it >= 1) & (it < RING + 1))
        def _():
            gate_up(it - 1)

        @pl.when((it >= 2) & (it < RING + 2))
        def _():
            relay(act, ac_s, ac_r, it - 2, 2 * HID)

        @pl.when(it >= 3)
        def _():
            down(it - 3)

        return carry

    lax.fori_loop(0, RING + 3, step, 0)

    def returned(i, carry):
        arrived(ret.at[lax.rem(r2 + ahead(i), RING)], rt_r.at[i])
        return carry

    lax.fori_loop(1, RING, returned, 0)

    for h in range(2):
        rows = ret[:, h * HALF : (h + 1) * HALF, :].reshape(RING * HALF, QD)
        both = jnp.dot(comb[h], rows, preferred_element_type=F32)
        sums = (both[: TOKS // 2] + both[TOKS // 2 :]).astype(BF)
        part[h * (RING // 2) : (h + 1) * (RING // 2)] = sums.reshape(RING // 2, XN * ROWS, QD)
    for d in range(1, RING):
        to = lax.rem(r1 + d, RING)
        rcopy(part.at[to], parts.at[r1], rs_s.at[d], rs_r.at[d], ring1(to)).start()
    total = part[r1].astype(F32)
    for d in range(1, RING):
        at = lax.rem(r1 + RING - d, RING)
        arrived(parts.at[at], rs_r.at[d])
        total = total + parts[at].astype(F32)
    mix[...] = total.astype(BF)
    for d in range(1, XN):
        to = lax.rem(x + d, XN)
        rcopy(mix.at[block(to)], fin.at[:, band(x, QD)], xb_s.at[d], xb_r.at[d], along_x(to)).start()
    fin[:, band(x, QD)] = mix[block(x), :]
    for d in range(1, XN):
        arrived(fin.at[:, band(lax.rem(x + XN - d, XN), QD)], xb_r.at[d])
    out[...] = (hid[...] + fin[...].astype(F32)).astype(BF)

    for k, mine in enumerate((wg, wu, wd)):
        sent(mine, w_s.at[k])
    for d in range(1, XN):
        sent(nrm.at[:, band(x, QD)], xa_s.at[d])
        sent(mix.at[block(x)], xb_s.at[d])
    for d in range(1, RING):
        sent(meta, m_s.at[d])
        sent(gath.at[r1], g_s.at[d])
        sent(part.at[r1], rs_s.at[d])

    def drain(i, carry):
        @pl.when(i > 0)
        def _():
            sent(disp.at[i], d_s.at[i])
            sent(back.at[i], rt_s.at[i])

        for k in range(2):
            sent(xg.at[i, :, band(x, QD)], xg_s.at[i, k])
            sent(act.at[i, :, band(x, 2 * HID)], ac_s.at[i, k])
            sent(xg.at[i, pl.ds(0, HALF), band(x, QD)], xg_s.at[i, 2 + k])
            sent(act.at[i, pl.ds(0, HALF), band(x, 2 * HID)], ac_s.at[i, 2 + k])
        return carry

    lax.fori_loop(0, RING, drain, 0)


def experts(normed, hidden_sum, meta, w_gate, w_up, w_down):
    dma = pltpu.SemaphoreType.DMA
    vmem = pltpu.VMEM
    return pl.pallas_call(
        moe_kernel,
        out_shape=jax.ShapeDtypeStruct((ROWS, D), BF),
        in_specs=[pl.BlockSpec(memory_space=pltpu.VMEM)] * 6,
        out_specs=pl.BlockSpec(memory_space=pltpu.VMEM),
        scratch_shapes=[
            vmem((D, HID), BF),
            vmem((D, HID), BF),
            vmem((XN * 2 * HID, QD // 2), BF),
            vmem((RING, 2 * TOP, 128), F32),
            vmem((RING, XN * ROWS, QD), BF),
            vmem((RING, TOKS), F32),
            vmem((RING, TOKS), F32),
            vmem((RING, 2, HALF, TOKS // 2), BF),
            vmem((RING * HALF, TOKS // 2), F32),
            vmem((2, TOKS, RING * HALF), BF),
            vmem((RING, SLOTS, QD), BF),
            vmem((RING, SLOTS, D), BF),
            vmem((RING, SLOTS, XN * 2 * HID), BF),
            vmem((RING, SLOTS, QD), BF),
            vmem((RING, SLOTS, QD), BF),
            vmem((RING, XN * ROWS, QD), BF),
            vmem((RING, XN * ROWS, QD), BF),
            vmem((XN * ROWS, QD), BF),
            vmem((ROWS, D), BF),
            dma((3,)), dma((3,)),
            dma((RING,)), dma((RING,)),
            dma((XN,)), dma((XN,)),
            dma((RING,)), dma((RING,)),
            dma((RING,)), dma((RING,)),
            dma((RING, 4)), dma((RING, 4)),
            dma((RING, 4)), dma((RING, 4)),
            dma((RING,)), dma((RING,)),
            dma((RING,)), dma((RING,)),
            dma((XN,)), dma((XN,)),
        ],
        compiler_params=pltpu.CompilerParams(
            collective_id=0, has_side_effects=True, vmem_limit_bytes=50 * 1024 * 1024
        ),
        name="experts",
    )(normed, hidden_sum, meta, w_gate, w_up, w_down)


def shards(
    queries,
    keys,
    values,
    segments,
    out_weight,
    residual,
    norm_gain,
    picks,
    route_weights,
    w_gate,
    w_up,
    w_down,
):
    tensor_index = lax.axis_index("tensor")
    group_tokens = queries.shape[0]
    local_heads = queries.shape[1] // HD
    head_ids = tensor_index * local_heads + jnp.arange(local_heads, dtype=jnp.int32)
    choose = (
        head_ids[:, None] // (HEADS // KVH) == jnp.arange(KVH, dtype=jnp.int32)[None, :]
    ).astype(jnp.bfloat16)
    key_heads = jnp.einsum(
        "skd,hk->shd",
        keys.reshape(group_tokens, KVH, HD),
        choose,
        preferred_element_type=jnp.float32,
    ).astype(jnp.bfloat16)
    value_heads = jnp.einsum(
        "skd,hk->shd",
        values.reshape(group_tokens, KVH, HD),
        choose,
        preferred_element_type=jnp.float32,
    ).astype(jnp.bfloat16)
    query_heads = queries.reshape(group_tokens, local_heads, HD)
    scores = jnp.einsum(
        "thd,shd->hts", query_heads, key_heads, preferred_element_type=jnp.float32
    ) * (1.0 / math.sqrt(HD))
    position = jnp.arange(group_tokens, dtype=jnp.int32)
    documents = segments[0]
    visible = (documents[:, None] == documents[None, :]) & (position[None, :] <= position[:, None])
    scores = jnp.where(visible[None], scores, -1e30)
    row_top = jnp.max(scores, axis=2, keepdims=True)
    expanded = jnp.exp(scores - row_top)
    weights_bf = (expanded / jnp.sum(expanded, axis=2, keepdims=True)).astype(jnp.bfloat16)
    context = jnp.einsum(
        "hts,shd->thd", weights_bf, value_heads, preferred_element_type=jnp.float32
    ).astype(jnp.bfloat16)
    context = context.reshape(group_tokens, local_heads * HD)
    attended = lax.psum_scatter(
        jnp.dot(context, out_weight, preferred_element_type=jnp.float32).astype(jnp.bfloat16),
        "tensor",
        scatter_dimension=0,
        tiled=True,
    ).astype(jnp.float32)
    hidden_sum = residual.astype(jnp.float32) + attended
    stream = hidden_sum.astype(jnp.bfloat16)
    mean_square = jnp.mean(hidden_sum * hidden_sum, axis=1, keepdims=True)
    normed = (hidden_sum * lax.rsqrt(mean_square + 1e-06) * norm_gain[None, :]).astype(jnp.bfloat16)

    core = lax.rem(tensor_index, 2)
    routing = jnp.concatenate([picks.astype(F32), route_weights], axis=1)
    routing = routing.reshape(XN, 2, ROWS, 2 * TOP)
    routing = jnp.where(core == 0, routing[:, 0], routing[:, 1]).reshape(XN * ROWS, 2 * TOP).T
    meta = jnp.concatenate([routing, routing], axis=1)
    layer_out = experts(normed, hidden_sum, meta, w_gate[0], w_up[0], w_down[0])
    return (stream, layer_out)


def solution(mesh):
    in_specs = (
        P("expert", "tensor"),
        P("expert", None),
        P("expert", None),
        P("expert", None),
        P("tensor", None),
        P(("expert", "tensor"), None),
        P(),
        P("expert", None),
        P("expert", None),
        P("expert", None, "tensor"),
        P("expert", None, "tensor"),
        P("expert", None, "tensor"),
    )
    out_specs = (P(("expert", "tensor"), None), P(("expert", "tensor"), None))
    return jax.shard_map(shards, mesh=mesh, in_specs=in_specs, out_specs=out_specs, check_vma=False)
```
